32 devices in a mesh: groups: 2 (over x), seq: 16 (over z, y, core).
Axes of the slice: x: 2, y: 2, z: 4, core: 2. Of those that a mesh axis runs over, the one named last changes fastest.
Arguments:
- queries: bfloat16 [1024, 2048], P(('groups', 'seq')), parts along dimension 0, may hold values from -2048 to 2048
- new_keys: bfloat16 [1024, 512], P(('groups', 'seq')), parts along dimension 0, may hold values from -16 to 16
- new_values: bfloat16 [1024, 512], P(('groups', 'seq')), parts along dimension 0, may hold values from -6 to 6
- keys: bfloat16 [131072, 512], P(('groups', 'seq')), parts along dimension 0, may hold values from -16 to 16
- values: bfloat16 [131072, 512], P(('groups', 'seq')), parts along dimension 0, may hold values from -6 to 6
- page_list: int32 [256, 3], P(('groups', 'seq')), parts along dimension 0, may hold values from 0 to 15, as said below
- out_weight: bfloat16 [2048, 4096], P(None, 'seq'), may hold values from -0.125 to 0.125
Outputs:
- projected: bfloat16 [1024, 4096], P(('groups', 'seq')), parts along dimension 0
The draws below stay inside these ranges and needn't reach their ends.
There are 2 independent parts, one for each index of `groups`. The reference program is written for one: setup_inputs(seed, part) draws one part's arguments, and reference() takes and returns one part's arrays. A program takes and returns all parts, laid end to end along the dimension named above; an argument that names none is the same for every part. Nothing has to cross between parts.
Inputs may be any that keep to these rules, and one draw needn't show every extreme that they name: `page_list`: the 3 pages of a tile are distinct. Among the 8 tiles of one index of seq (tiles 8 * i to 8 * (i + 1) - 1) no page is listed more than 3 times, and some page is listed exactly 3 times by the tiles of every index.
All inputs are finite; a program needn't handle non-finite values.
Results may differ from the reference program's by a relative error of at most 0.0058.
Values may be sent and summed in bfloat16 or wider, within the bound.
A program may use at most 192 MiB of HBM per device.

```python
import math
import jax
import jax.numpy as jnp
from jax import lax

D = 4096
HQ = 16
KVH = 4
HD = 128
PAGE = 4096
QT = 4
TOPK = 3
TILES_DEV = 8
TILES = 128
TOKENS = 512
STORED_BLOCKS = 16
CAP = 3


def page_table(base_key):
    block_directory_seed = jax.random.fold_in(base_key, 11)
    extra_credit_seed, favourite_block_seed, logit_matrix_seed, sequence_rank_seed, shift_amount_seed = jax.random.split(block_directory_seed, 5)
    blocks = TILES // TILES_DEV
    candidates = STORED_BLOCKS * CAP
    ident = jnp.arange(candidates, dtype=jnp.int32)
    owner_page = ident // CAP
    hottest = jax.random.randint(favourite_block_seed, (), 0, STORED_BLOCKS)
    favour_increment = jax.random.randint(extra_credit_seed, (STORED_BLOCKS,), 0, 4) * 1024
    random_part = jax.random.randint(logit_matrix_seed, (blocks, candidates), 0, 1024)
    priority = random_part + favour_increment[owner_page][None, :] + jnp.where(owner_page == hottest, 8192, 0)[None, :]
    priority = priority * candidates + ident[None, :]
    ignored, picked = lax.top_k(priority, TILES_DEV * TOPK)
    picked = jnp.sort(picked, axis=1)
    listed = (picked // CAP).reshape(blocks, TOPK, TILES_DEV).transpose(0, 2, 1)
    orders = jax.vmap(lambda one_key: jax.random.permutation(one_key, TILES_DEV))(jax.random.split(sequence_rank_seed, blocks))
    listed = jnp.take_along_axis(listed, orders[:, :, None], axis=1)
    turned = (jnp.arange(TOPK)[None, None, :] + jax.random.randint(shift_amount_seed, (blocks, TILES_DEV, 1), 0, TOPK)) % TOPK
    listed = jnp.take_along_axis(listed, turned, axis=2)
    return listed.reshape(TILES, TOPK).astype(jnp.int32)


def float_fields(base_key):
    field_key = jax.random.fold_in(base_key, 23)
    subkeys = jax.random.split(field_key, 3)
    rows_all = STORED_BLOCKS * PAGE
    cached = jax.random.truncated_normal(subkeys[0], -6.0, 6.0, (rows_all, KVH * HD), jnp.float32)
    fresh = 1.8 * jax.random.truncated_normal(subkeys[1], -6.0, 6.0, (TILES * QT, KVH * HD), jnp.float32)
    asked = 2.5 * jax.random.truncated_normal(subkeys[2], -6.0, 6.0, (TILES * QT, HQ * HD), jnp.float32)
    return (cached, fresh, asked)


def draw_page_list(key, part):
    return page_table(key)


def draw_keys(key, part):
    return float_fields(key)[0].astype(jnp.bfloat16)


def draw_new_keys(key, part):
    return float_fields(key)[1].astype(jnp.bfloat16)


def draw_queries(key, part):
    return float_fields(key)[2].astype(jnp.bfloat16)


def block_scale(key, shape, shards, low, largest):
    def one(position, parts):
        steps = jax.random.uniform(jax.random.fold_in(jax.random.fold_in(key, 6), position), (parts,), jnp.float32, low / len(shards), largest / len(shards))
        return jnp.repeat(jnp.exp(steps), shape[position] // parts).reshape((-1,) + (1,) * (len(shape) - position - 1))

    gain = one(*shards[0])
    for cut in shards[1:]:
        gain = gain * one(*cut)
    return gain


def scatter_about(key, extent, deviation, limit, cuts=(), kind=jnp.bfloat16):
    factor_of = block_scale(key, extent, cuts, -0.22, 0.18) if cuts else 1.0
    values = jax.random.normal(key, extent, jnp.float32) * deviation * factor_of
    return jnp.minimum(jnp.maximum(values, -limit), limit).astype(kind)


def setup_inputs(seed: int = 0, part: int = 0) -> dict:
    splits = jax.random.split(jax.random.key(seed), 8)
    own_keys = jax.random.split(jax.random.fold_in(splits[7], part), 8)
    return {
        "queries": draw_queries(jax.random.fold_in(jax.random.fold_in(splits[7], part), 71), part),
        "new_keys": draw_new_keys(jax.random.fold_in(jax.random.fold_in(splits[7], part), 71), part),
        "new_values": scatter_about(own_keys[2], (TOKENS, KVH * HD), 1.0, 6.0, ((0, 16),)),
        "keys": draw_keys(jax.random.fold_in(jax.random.fold_in(splits[7], part), 71), part),
        "values": scatter_about(own_keys[4], (STORED_BLOCKS * PAGE, KVH * HD), 1.0, 6.0, ((0, 16),)),
        "page_list": draw_page_list(jax.random.fold_in(jax.random.fold_in(splits[7], part), 71), part),
        "out_weight": scatter_about(splits[6], (HQ * HD, D), (HQ * HD) ** -0.5, 0.125, ((1, 16),)),
    }


def partial_softmax(asked, cached_keys, cached_values, allowed):
    row_count = asked.shape[0]
    per_group = HQ // KVH
    query_full = asked.astype(jnp.float32).reshape(row_count, KVH, per_group, HD)
    key_full = cached_keys.astype(jnp.float32).reshape(-1, KVH, HD)
    value_full = cached_values.astype(jnp.float32).reshape(-1, KVH, HD)
    scores = jnp.einsum('rgjd,lgd->rgjl', query_full, key_full, precision=lax.Precision.HIGHEST) / math.sqrt(HD)
    if allowed is not None:
        scores = jnp.where(allowed[:, None, None, :], scores, -jnp.inf)
    highest = lax.optimization_barrier(jnp.max(scores, axis=-1))
    weights = jnp.exp(scores - highest[..., None])
    summed = lax.optimization_barrier(jnp.sum(weights, axis=-1))
    rounded = lax.optimization_barrier(weights.astype(jnp.bfloat16)).astype(jnp.float32)
    mixed = jnp.einsum('rgjl,lgd->rgjd', rounded, value_full, precision=lax.Precision.HIGHEST) / summed[..., None]
    return (mixed.reshape(row_count, HQ, HD), highest.reshape(row_count, HQ), summed.reshape(row_count, HQ))

def reference(queries, new_keys, new_values, keys, values, page_list, out_weight):

    def one_tile(tile):
        start = (tile * QT).astype(jnp.int32)
        asked = lax.dynamic_slice_in_dim(queries, start, QT, 0)
        fresh_keys = lax.dynamic_slice_in_dim(new_keys, start, QT, 0)
        fresh_values = lax.dynamic_slice_in_dim(new_values, start, QT, 0)
        causal = jnp.arange(QT)[:, None] >= jnp.arange(QT)[None, :]
        own_out, own_max, own_total = partial_softmax(asked, fresh_keys, fresh_values, causal)
        outputs = [own_out]
        maxima = [own_max]
        totals = [own_total]
        for listed in range(TOPK):
            first = (page_list[tile, listed] * PAGE).astype(jnp.int32)
            page_keys = lax.dynamic_slice_in_dim(keys, first, PAGE, 0)
            page_values = lax.dynamic_slice_in_dim(values, first, PAGE, 0)
            page_out, page_max, page_total = partial_softmax(asked, page_keys, page_values, None)
            page_out = lax.optimization_barrier(page_out.astype(jnp.bfloat16)).astype(jnp.float32)
            outputs.append(page_out)
            maxima.append(page_max)
            totals.append(page_total)
        all_max = jnp.stack(maxima)
        all_total = jnp.stack(totals)
        all_out = jnp.stack(outputs)
        top = lax.optimization_barrier(jnp.max(all_max, axis=0))
        factors = all_total * jnp.exp(all_max - top[None])
        numer = lax.optimization_barrier(jnp.sum(factors[..., None] * all_out, axis=0))
        denom = lax.optimization_barrier(jnp.sum(factors, axis=0))
        return (numer / denom[..., None]).reshape(QT, HQ * HD).astype(jnp.bfloat16)
    attended = lax.map(one_tile, jnp.arange(TILES, dtype=jnp.int32)).reshape(TILES * QT, HQ * HD)
    return jnp.dot(attended, out_weight, preferred_element_type=jnp.float32).astype(jnp.bfloat16)
```

```python
import functools
import math

import jax
import jax.numpy as jnp
from jax import lax
from jax.experimental import pallas as pl
from jax.experimental.pallas import tpu as pltpu
from jax.sharding import PartitionSpec as P

HQ = 16
KVH = 4
HD = 128
PER = HQ // KVH
SCALE = 1.0 / math.sqrt(HD)
LOG2E = math.log2(math.e)


def flash_rows(q, k_ref, v_ref, chunk):
    nt = (((1,), (1,)), ((), ()))
    count = k_ref.shape[0] // chunk
    score = lambda c: lax.dot_general(
        q, k_ref[c * chunk : (c + 1) * chunk, :], nt, preferred_element_type=jnp.float32
    )
    high = total = acc = None
    nxt = score(0)
    for c in range(count):
        s = nxt
        if c + 1 < count:
            nxt = score(c + 1)
        m = jnp.max(s, axis=1, keepdims=True)
        new = m if c == 0 else jnp.maximum(high, m)
        w = jnp.exp2((s - new) * (SCALE * LOG2E))
        t = jnp.sum(w, axis=1, keepdims=True)
        o = jnp.dot(
            w.astype(jnp.bfloat16),
            v_ref[c * chunk : (c + 1) * chunk, :],
            preferred_element_type=jnp.float32,
        )
        if c == 0:
            total, acc = t, o
        else:
            fix = jnp.exp2((high - new) * (SCALE * LOG2E))
            total = total * fix + t
            acc = acc * fix + o
        high = new
    return acc / total, high * SCALE, total


def page_kernel(block, chunk, q_ref, k_ref, v_ref, out_ref, stat_ref):
    @pl.loop(0, q_ref.shape[1] // block)
    def _(i):
        rows = pl.ds(pl.multiple_of(i * block, block), block)
        out, high, total = flash_rows(q_ref[0, rows, :], k_ref, v_ref, chunk)
        out_ref[0, rows, :] = out.astype(out_ref.dtype)
        stat_ref[0, rows, 0:1] = high
        stat_ref[0, rows, 1:2] = total


def page_attention(q, keys, values):
    rows = q.shape[1]
    page = keys.shape[0]
    block = next(b for b in (256, 128, 64, 16) if rows % b == 0)
    chunk = next(c for c in (1024, 512, page) if page % c == 0)
    return pl.pallas_call(
        functools.partial(page_kernel, block, chunk),
        grid=(KVH,),
        in_specs=[
            pl.BlockSpec((1, rows, HD), lambda g: (g, 0, 0)),
            pl.BlockSpec((page, HD), lambda g: (0, g)),
            pl.BlockSpec((page, HD), lambda g: (0, g)),
        ],
        out_specs=[
            pl.BlockSpec((1, rows, HD), lambda g: (g, 0, 0)),
            pl.BlockSpec((1, rows, 2), lambda g: (g, 0, 0)),
        ],
        out_shape=[
            jax.ShapeDtypeStruct((KVH, rows, HD), jnp.bfloat16),
            jax.ShapeDtypeStruct((KVH, rows, 2), jnp.float32),
        ],
        compiler_params=pltpu.CompilerParams(vmem_limit_bytes=40 * 1024 * 1024),
    )(q, keys, values)


def shards(queries, new_keys, new_values, keys, values, page_list, out_weight):
    members = lax.axis_size("seq")
    tiles, width = page_list.shape
    row_total, features = queries.shape
    rows = row_total // tiles
    unit = rows * PER
    capacity = max(1, 2 * tiles * width // members)
    slots = members * capacity
    ids = jnp.arange(tiles)
    before = ids[None, :] < ids[:, None]
    matches = page_list[:, :, None, None] == page_list[None, None, :, :]
    ranking = jnp.sum(matches & before[:, None, :, None], axis=(2, 3))
    slot_index = page_list * capacity + ranking
    placing = jnp.any(
        slot_index[:, :, None] == jnp.arange(slots, dtype=jnp.int32)[None, None, :], axis=1
    ).astype(jnp.bfloat16)
    asked = queries.reshape(tiles, rows, KVH, PER, HD).transpose(0, 2, 1, 3, 4)
    asked = asked.reshape(tiles, KVH, unit, HD)
    outgoing = lax.dot_general(
        placing,
        asked.reshape(tiles, -1),
        (((0,), (0,)), ((), ())),
        preferred_element_type=jnp.float32,
    ).astype(jnp.bfloat16)
    outgoing = outgoing.reshape(members, capacity, KVH, unit, HD)
    incoming = lax.all_to_all(outgoing, "seq", split_axis=0, concat_axis=0, tiled=True)
    incoming = incoming.transpose(2, 0, 1, 3, 4).reshape(KVH, slots * unit, HD)
    out, stat = page_attention(incoming, keys, values)
    out = out.reshape(KVH, members, capacity, unit, HD).transpose(1, 2, 0, 3, 4)
    stat = stat.reshape(KVH, members, capacity, unit, 2).transpose(1, 2, 0, 3, 4)
    stat = stat.reshape(members, capacity, KVH * unit * 2)
    got = lax.all_to_all(out, "seq", split_axis=0, concat_axis=0, tiled=True)
    got_stat = lax.all_to_all(stat, "seq", split_axis=0, concat_axis=0, tiled=True)
    a = asked.reshape(tiles, KVH, rows, PER, HD).astype(jnp.float32)
    nk = new_keys.reshape(tiles, rows, KVH, HD).transpose(0, 2, 1, 3).astype(jnp.float32)
    nv = new_values.reshape(tiles, rows, KVH, HD).transpose(0, 2, 1, 3).astype(jnp.float32)
    own_s = jnp.sum(a[:, :, :, :, None, :] * nk[:, :, None, None, :, :], axis=-1) * SCALE
    causal = jnp.arange(rows)[:, None] >= jnp.arange(rows)[None, :]
    own_s = jnp.where(causal[None, None, :, None, :], own_s, -jnp.inf)
    own_max = jnp.max(own_s, axis=-1)
    own_w = jnp.exp(own_s - own_max[..., None])
    own_total = jnp.sum(own_w, axis=-1)
    own_w = own_w.astype(jnp.bfloat16).astype(jnp.float32)
    own_sum = jnp.sum(own_w[..., None] * nv[:, :, None, None, :, :], axis=4)

    pick = slot_index[:, :, None] == jnp.arange(slots, dtype=jnp.int32)
    chosen = lax.dot_general(
        pick.reshape(tiles * width, slots).astype(jnp.bfloat16),
        got.reshape(slots, KVH * unit * HD),
        (((1,), (0,)), ((), ())),
        preferred_element_type=jnp.float32,
    ).reshape(tiles, width, KVH, rows, PER, HD)
    got_stat = got_stat.reshape(slots, KVH, rows, PER, 2)
    chosen_stat = jnp.sum(
        jnp.where(pick[..., None], got_stat.reshape(slots, -1)[None, None], 0.0), axis=2
    ).reshape(tiles, width, KVH, rows, PER, 2)
    chosen_max = chosen_stat[..., 0]
    chosen_total = chosen_stat[..., 1]
    top = jnp.maximum(own_max, jnp.max(chosen_max, axis=1))
    own_exp = jnp.exp(own_max - top)
    factor = chosen_total * jnp.exp(chosen_max - top[:, None])
    denom = own_exp * own_total + jnp.sum(factor, axis=1)
    numer = own_exp[..., None] * own_sum + jnp.sum(factor[..., None] * chosen, axis=1)
    attended = (numer / denom[..., None]).astype(jnp.bfloat16)
    attended = attended.transpose(0, 2, 1, 3, 4).reshape(row_total, features)
    everyone = lax.all_gather(attended, "seq", axis=0, tiled=True)
    columns = jnp.dot(everyone, out_weight, preferred_element_type=jnp.float32)
    columns = columns.astype(jnp.bfloat16).reshape(members, row_total, -1)
    mine = lax.all_to_all(columns, "seq", split_axis=0, concat_axis=0, tiled=True)
    return mine.transpose(1, 0, 2).reshape(row_total, -1)


def solution(mesh):
    rows = P(("groups", "seq"), None)
    return jax.shard_map(
        shards,
        mesh=mesh,
        in_specs=(rows, rows, rows, rows, rows, rows, P(None, "seq")),
        out_specs=rows,
        check_vma=False,
    )
```

```python
import functools
import math

import jax
import jax.numpy as jnp
from jax import lax
from jax.experimental import pallas as pl
from jax.experimental.pallas import tpu as pltpu
from jax.sharding import PartitionSpec as P

HQ = 16
KVH = 4
HD = 128
PER = HQ // KVH
SCALE = 1.0 / math.sqrt(HD)
LOG2E = math.log2(math.e)


def flash_rows(q, k_ref, v_ref, chunk):
    nt = (((1,), (1,)), ((), ()))
    count = k_ref.shape[0] // chunk
    score = lambda c: lax.dot_general(
        q, k_ref[c * chunk : (c + 1) * chunk, :], nt, preferred_element_type=jnp.float32
    )
    high = total = acc = None
    nxt = score(0)
    for c in range(count):
        s = nxt
        if c + 1 < count:
            nxt = score(c + 1)
        m = jnp.max(s, axis=1, keepdims=True)
        new = m if c == 0 else jnp.maximum(high, m)
        w = jnp.exp2((s - new) * (SCALE * LOG2E))
        t = jnp.sum(w, axis=1, keepdims=True)
        o = jnp.dot(
            w.astype(jnp.bfloat16),
            v_ref[c * chunk : (c + 1) * chunk, :],
            preferred_element_type=jnp.float32,
        )
        if c == 0:
            total, acc = t, o
        else:
            fix = jnp.exp2((high - new) * (SCALE * LOG2E))
            total = total * fix + t
            acc = acc * fix + o
        high = new
    return acc / total, high * SCALE, total


def page_kernel(block, chunk, q_ref, k_ref, v_ref, out_ref, stat_ref):
    @pl.loop(0, q_ref.shape[1] // block)
    def _(i):
        rows = pl.ds(pl.multiple_of(i * block, block), block)
        out, high, total = flash_rows(q_ref[0, rows, :], k_ref, v_ref, chunk)
        out_ref[0, rows, :] = out.astype(out_ref.dtype)
        stat_ref[0, rows, 0:1] = high
        stat_ref[0, rows, 1:2] = total


def page_attention(q, keys, values):
    rows = q.shape[1]
    page = keys.shape[0]
    block = next(b for b in (256, 128, 64, 16) if rows % b == 0)
    chunk = next(c for c in (1024, 512, page) if page % c == 0)
    return pl.pallas_call(
        functools.partial(page_kernel, block, chunk),
        grid=(KVH,),
        in_specs=[
            pl.BlockSpec((1, rows, HD), lambda g: (g, 0, 0)),
            pl.BlockSpec((page, HD), lambda g: (0, g)),
            pl.BlockSpec((page, HD), lambda g: (0, g)),
        ],
        out_specs=[
            pl.BlockSpec((1, rows, HD), lambda g: (g, 0, 0)),
            pl.BlockSpec((1, rows, 2), lambda g: (g, 0, 0)),
        ],
        out_shape=[
            jax.ShapeDtypeStruct((KVH, rows, HD), jnp.bfloat16),
            jax.ShapeDtypeStruct((KVH, rows, 2), jnp.float32),
        ],
        compiler_params=pltpu.CompilerParams(vmem_limit_bytes=40 * 1024 * 1024),
    )(q, keys, values)


def project_kernel(n, att_ref, w_ref, out_ref, held, result, got, r_send, r_recv, l_send, l_recv, s_send, s_recv, p_send, p_recv):
    me = lax.axis_index("seq")
    rows = att_ref.shape[0]
    wide = w_ref.shape[1]
    chips = n // 2
    core = lax.rem(me, 2)
    chip = me // 2
    half = (chips + 1) // 2
    place = jnp.where(lax.rem(chip, 2) == 0, chip // 2, chips - 1 - chip // 2)

    def chip_at(p):
        p = lax.rem(p + 2 * chips, chips)
        return jnp.where(p < half, 2 * p, 2 * (chips - 1 - p) + 1)

    sibling = chip * 2 + (1 - core)
    right = chip_at(place + 1) * 2 + core
    left = chip_at(place - 1) * 2 + core

    barrier = pltpu.get_barrier_semaphore()

    @pl.loop(0, n - 1)
    def _(i):
        pl.semaphore_signal(
            barrier, inc=1, device_id={"seq": lax.rem(me + 1 + i, n)},
            device_id_type=pl.DeviceIdType.MESH,
        )

    held[pl.ds(pl.multiple_of(me * rows, rows), rows), :] = att_ref[...]
    pl.semaphore_wait(barrier, n - 1)

    def block(d):
        return held.at[pl.ds(pl.multiple_of(d * rows, rows), rows), :]

    def move(d, to, send, recv):
        return pltpu.make_async_remote_copy(
            src_ref=block(d), dst_ref=block(d), send_sem=send, recv_sem=recv,
            device_id={"seq": to}, device_id_type=pl.DeviceIdType.MESH,
        )

    def give(d, slot):
        return pltpu.make_async_remote_copy(
            src_ref=result.at[pl.ds(pl.multiple_of(d * rows, rows), rows), :],
            dst_ref=got.at[pl.ds(pl.multiple_of(me * rows, rows), rows), :],
            send_sem=p_send.at[slot], recv_sem=p_recv.at[me],
            device_id={"seq": d}, device_id_type=pl.DeviceIdType.MESH,
        )

    rights, lefts = chips // 2, (chips - 1) // 2
    started = []

    def project(c):
        return jnp.dot(
            held[pl.ds(pl.multiple_of(c * 2 * rows, 2 * rows), 2 * rows), :], w_ref[...],
            preferred_element_type=jnp.float32,
        ).astype(jnp.bfloat16)

    def finish(k, c):
        move(c * 2 + (1 - core), sibling, s_send.at[k], s_recv.at[k]).wait_recv()
        result[pl.ds(pl.multiple_of(c * 2 * rows, 2 * rows), 2 * rows), :] = project(c)
        if k == 0:
            mine = result[pl.ds(pl.multiple_of(me * rows, rows), rows), :]
            got[pl.ds(pl.multiple_of(me * rows, rows), rows), :] = mine
            sent = [give(sibling, 0)]
        else:
            sent = [give(c * 2, 2 * k), give(c * 2 + 1, 2 * k + 1)]
        for copy in sent:
            copy.start()
        started.extend(sent)

    def launch(copy):
        copy.start()
        started.append(copy)

    def step_right(s):
        launch(move(chip_at(place - s) * 2 + core, right, r_send.at[s], r_recv.at[s]))

    def step_left(s):
        launch(move(chip_at(place + s) * 2 + core, left, l_send.at[s], l_recv.at[s]))

    step_right(0)
    if lefts:
        step_left(0)
    launch(move(me, sibling, s_send.at[0], s_recv.at[0]))
    waiting = [(0, chip)]
    k = 1
    for s in range(rights):
        c = chip_at(place - 1 - s)
        move(c * 2 + core, right, r_send.at[s], r_recv.at[s]).wait_recv()
        if s + 1 < rights:
            step_right(s + 1)
        launch(move(c * 2 + core, sibling, s_send.at[k], s_recv.at[k]))
        now = [(k, c)]
        k += 1
        if s < lefts:
            c = chip_at(place + 1 + s)
            move(c * 2 + core, left, l_send.at[s], l_recv.at[s]).wait_recv()
            if s + 1 < lefts:
                step_left(s + 1)
            launch(move(c * 2 + core, sibling, s_send.at[k], s_recv.at[k]))
            now.append((k, c))
            k += 1
        for job in waiting:
            finish(*job)
        waiting = now
    for job in waiting:
        finish(*job)
    for copy in started:
        copy.wait_send()

    @pl.loop(0, n - 1)
    def _(i):
        d = lax.rem(me + 1 + i, n)
        pltpu.make_async_remote_copy(
            src_ref=result.at[pl.ds(0, rows), :],
            dst_ref=got.at[pl.ds(pl.multiple_of(d * rows, rows), rows), :],
            send_sem=p_send.at[1], recv_sem=p_recv.at[d],
            device_id={"seq": d}, device_id_type=pl.DeviceIdType.MESH,
        ).wait_recv()

    for d in range(n):
        out_ref[:, d * wide : (d + 1) * wide] = got[d * rows : (d + 1) * rows, :]


def project(attended, out_weight):
    n = lax.axis_size("seq")
    rows, features = attended.shape
    wide = out_weight.shape[1]
    chips = n // 2
    vmem = pl.BlockSpec(memory_space=pltpu.VMEM)
    dma = pltpu.SemaphoreType.DMA
    return pl.pallas_call(
        functools.partial(project_kernel, n),
        out_shape=jax.ShapeDtypeStruct((rows, n * wide), jnp.bfloat16),
        in_specs=[vmem, vmem],
        out_specs=vmem,
        scratch_shapes=[
            pltpu.VMEM((n * rows, features), jnp.bfloat16),
            pltpu.VMEM((n * rows, wide), jnp.bfloat16),
            pltpu.VMEM((n * rows, wide), jnp.bfloat16),
            dma((chips,)), dma((chips,)), dma((chips,)), dma((chips,)),
            dma((chips,)), dma((chips,)), dma((n,)), dma((n,)),
        ],
        compiler_params=pltpu.CompilerParams(
            collective_id=0, has_side_effects=True, vmem_limit_bytes=40 * 1024 * 1024
        ),
    )(attended, out_weight)


def shards(queries, new_keys, new_values, keys, values, page_list, out_weight):
    members = lax.axis_size("seq")
    tiles, width = page_list.shape
    row_total, features = queries.shape
    rows = row_total // tiles
    unit = rows * PER
    capacity = max(1, 2 * tiles * width // members)
    slots = members * capacity
    ids = jnp.arange(tiles)
    before = ids[None, :] < ids[:, None]
    matches = page_list[:, :, None, None] == page_list[None, None, :, :]
    ranking = jnp.sum(matches & before[:, None, :, None], axis=(2, 3))
    slot_index = page_list * capacity + ranking
    placing = jnp.any(
        slot_index[:, :, None] == jnp.arange(slots, dtype=jnp.int32)[None, None, :], axis=1
    ).astype(jnp.bfloat16)
    asked = queries.reshape(tiles, rows, KVH, PER, HD).transpose(0, 2, 1, 3, 4)
    asked = asked.reshape(tiles, KVH, unit, HD)
    outgoing = lax.dot_general(
        placing,
        asked.reshape(tiles, -1),
        (((0,), (0,)), ((), ())),
        preferred_element_type=jnp.float32,
    ).astype(jnp.bfloat16)
    outgoing = outgoing.reshape(members, capacity, KVH, unit, HD)
    incoming = lax.all_to_all(outgoing, "seq", split_axis=0, concat_axis=0, tiled=True)
    incoming = incoming.transpose(2, 0, 1, 3, 4).reshape(KVH, slots * unit, HD)
    out, stat = page_attention(incoming, keys, values)
    out = out.reshape(KVH, members, capacity, unit, HD).transpose(1, 2, 0, 3, 4)
    stat = stat.reshape(KVH, members, capacity, unit, 2).transpose(1, 2, 0, 3, 4)
    stat = stat.reshape(members, capacity, KVH * unit * 2)
    got = lax.all_to_all(out, "seq", split_axis=0, concat_axis=0, tiled=True)
    got_stat = lax.all_to_all(stat, "seq", split_axis=0, concat_axis=0, tiled=True)
    a = asked.reshape(tiles, KVH, rows, PER, HD).astype(jnp.float32)
    nk = new_keys.reshape(tiles, rows, KVH, HD).transpose(0, 2, 1, 3).astype(jnp.float32)
    nv = new_values.reshape(tiles, rows, KVH, HD).transpose(0, 2, 1, 3).astype(jnp.float32)
    own_s = jnp.sum(a[:, :, :, :, None, :] * nk[:, :, None, None, :, :], axis=-1) * SCALE
    causal = jnp.arange(rows)[:, None] >= jnp.arange(rows)[None, :]
    own_s = jnp.where(causal[None, None, :, None, :], own_s, -jnp.inf)
    own_max = jnp.max(own_s, axis=-1)
    own_w = jnp.exp(own_s - own_max[..., None])
    own_total = jnp.sum(own_w, axis=-1)
    own_w = own_w.astype(jnp.bfloat16).astype(jnp.float32)
    own_sum = jnp.sum(own_w[..., None] * nv[:, :, None, None, :, :], axis=4)

    pick = slot_index[:, :, None] == jnp.arange(slots, dtype=jnp.int32)
    chosen = lax.dot_general(
        pick.reshape(tiles * width, slots).astype(jnp.bfloat16),
        got.reshape(slots, KVH * unit * HD),
        (((1,), (0,)), ((), ())),
        preferred_element_type=jnp.float32,
    ).reshape(tiles, width, KVH, rows, PER, HD)
    got_stat = got_stat.reshape(slots, KVH, rows, PER, 2)
    chosen_stat = jnp.sum(
        jnp.where(pick[..., None], got_stat.reshape(slots, -1)[None, None], 0.0), axis=2
    ).reshape(tiles, width, KVH, rows, PER, 2)
    chosen_max = chosen_stat[..., 0]
    chosen_total = chosen_stat[..., 1]
    top = jnp.maximum(own_max, jnp.max(chosen_max, axis=1))
    own_exp = jnp.exp(own_max - top)
    factor = chosen_total * jnp.exp(chosen_max - top[:, None])
    denom = own_exp * own_total + jnp.sum(factor, axis=1)
    numer = own_exp[..., None] * own_sum + jnp.sum(factor[..., None] * chosen, axis=1)
    attended = (numer / denom[..., None]).astype(jnp.bfloat16)
    attended = attended.transpose(0, 2, 1, 3, 4).reshape(row_total, features)
    return project(attended, out_weight)


def solution(mesh):
    rows = P(("groups", "seq"), None)
    return jax.shard_map(
        shards,
        mesh=mesh,
        in_specs=(rows, rows, rows, rows, rows, rows, P(None, "seq")),
        out_specs=rows,
        check_vma=False,
    )
```

```python
import functools
import math

import jax
import jax.numpy as jnp
from jax import lax
from jax.experimental import pallas as pl
from jax.experimental.pallas import tpu as pltpu
from jax.sharding import PartitionSpec as P

HQ = 16
KVH = 4
HD = 128
PER = HQ // KVH
SCALE = 1.0 / math.sqrt(HD)
LOG2E = math.log2(math.e)


def flash_rows(q, k_ref, v_ref, chunk):
    nt = (((1,), (1,)), ((), ()))
    count = k_ref.shape[0] // chunk
    score = lambda c: lax.dot_general(
        q, k_ref[c * chunk : (c + 1) * chunk, :], nt, preferred_element_type=jnp.float32
    )
    high = total = acc = None
    nxt = score(0)
    for c in range(count):
        s = nxt
        if c + 1 < count:
            nxt = score(c + 1)
        m = jnp.max(s, axis=1, keepdims=True)
        new = m if c == 0 else jnp.maximum(high, m)
        w = jnp.exp2((s - new) * (SCALE * LOG2E))
        t = jnp.sum(w, axis=1, keepdims=True)
        o = jnp.dot(
            w.astype(jnp.bfloat16),
            v_ref[c * chunk : (c + 1) * chunk, :],
            preferred_element_type=jnp.float32,
        )
        if c == 0:
            total, acc = t, o
        else:
            fix = jnp.exp2((high - new) * (SCALE * LOG2E))
            total = total * fix + t
            acc = acc * fix + o
        high = new
    return acc / total, high * SCALE, total


def asked_kernel(
    n, group, chunk, q_ref, k_hbm, v_hbm, got, got_stat, asked, answer, stat, stat_out, k_buf, v_buf,
    kv_sem, q_send, q_recv, o_send, o_recv, t_send, t_recv,
):
    me = lax.axis_index("seq")
    unit = q_ref.shape[2]
    blocks = n // group
    mesh_id = pl.DeviceIdType.MESH

    def page(g, src, buf, which):
        return pltpu.make_async_copy(
            src.at[:, g * HD : (g + 1) * HD], buf.at[g], kv_sem.at[which, g]
        )

    for g in range(KVH):
        page(g, k_hbm, k_buf, 0).start()
        page(g, v_hbm, v_buf, 1).start()

    barrier = pltpu.get_barrier_semaphore()

    @pl.loop(0, n - 1)
    def _(i):
        pl.semaphore_signal(
            barrier, inc=1, device_id={"seq": lax.rem(me + 1 + i, n)}, device_id_type=mesh_id
        )

    for g in range(KVH):
        asked[g, pl.ds(me, 1)] = q_ref[g, pl.ds(me, 1)]
    pl.semaphore_wait(barrier, n - 1)

    def ask(g, d):
        return pltpu.make_async_remote_copy(
            src_ref=q_ref.at[g, d], dst_ref=asked.at[g, me],
            send_sem=q_send.at[g, d], recv_sem=q_recv.at[g, me],
            device_id={"seq": d}, device_id_type=mesh_id,
        )

    def asked_by(g, d):
        return pltpu.make_async_remote_copy(
            src_ref=q_ref.at[g, d], dst_ref=asked.at[g, d],
            send_sem=q_send.at[g, d], recv_sem=q_recv.at[g, d],
            device_id={"seq": d}, device_id_type=mesh_id,
        )

    def reply(g, d):
        return pltpu.make_async_remote_copy(
            src_ref=answer.at[g, d], dst_ref=got.at[g, me],
            send_sem=o_send.at[g, d], recv_sem=o_recv.at[g, me],
            device_id={"seq": d}, device_id_type=mesh_id,
        )

    def replied_by(g, d):
        return pltpu.make_async_remote_copy(
            src_ref=answer.at[g, d], dst_ref=got.at[g, d],
            send_sem=o_send.at[g, d], recv_sem=o_recv.at[g, d],
            device_id={"seq": d}, device_id_type=mesh_id,
        )

    def note(d, slot):
        return pltpu.make_async_remote_copy(
            src_ref=stat_out.at[d], dst_ref=got_stat.at[slot],
            send_sem=t_send.at[d], recv_sem=t_recv.at[slot],
            device_id={"seq": d}, device_id_type=mesh_id,
        )

    @pl.loop(0, KVH)
    def _(g):
        @pl.loop(0, n - 1)
        def _(i):
            ask(g, lax.rem(me + 1 + i, n)).start()

    lane = lax.broadcasted_iota(jnp.int32, (group, unit, 128), 2)
    row = lax.broadcasted_iota(jnp.int32, (group, unit, 128), 1)
    diagonal = lane == row

    def line(column):
        spread = jnp.broadcast_to(column, (group * unit, 128)).reshape(group, unit, 128)
        return jnp.sum(jnp.where(diagonal, spread, 0.0), axis=1)

    for g in range(KVH):
        page(g, k_hbm, k_buf, 0).wait()
        page(g, v_hbm, v_buf, 1).wait()

        @pl.loop(0, blocks)
        def _(i):
            first = pl.multiple_of(lax.rem(me // group + i, blocks) * group, group)

            @pl.loop(0, group)
            def _(j):
                @pl.when(first + j != me)
                def _():
                    asked_by(g, first + j).wait_recv()

            q = asked[g, pl.ds(first, group)].reshape(group * unit, HD)
            out, high, total = flash_rows(q, k_buf.at[g], v_buf.at[g], chunk)
            answer[g, pl.ds(first, group)] = out.astype(jnp.bfloat16).reshape(group, unit, HD)
            stat[2 * g, pl.ds(first, group), :] = line(high)
            stat[2 * g + 1, pl.ds(first, group), :] = line(total)

            @pl.loop(0, group)
            def _(j):
                @pl.when(first + j != me)
                def _():
                    reply(g, first + j).start()

    for d in range(n):
        stat_out[d] = stat[:, d, :]

    @pl.loop(0, n - 1)
    def _(i):
        note(lax.rem(me + 1 + i, n), me).start()

    for g in range(KVH):
        got[g, pl.ds(me, 1)] = answer[g, pl.ds(me, 1)]
    got_stat[pl.ds(me, 1)] = stat_out[pl.ds(me, 1)]

    @pl.loop(0, n - 1)
    def _(i):
        d = lax.rem(me + 1 + i, n)
        for g in range(KVH):
            ask(g, d).wait_send()
            reply(g, d).wait_send()
            replied_by(g, d).wait_recv()
        note(d, d).wait_recv()
        note(d, me).wait_send()


def page_answers(q, keys, values):
    n = lax.axis_size("seq")
    unit = q.shape[2]
    page = keys.shape[0]
    group = next(b for b in (16, 8, 4, 2, 1) if n % b == 0 and b * unit <= 384)
    chunk = next(c for c in (1024, 512, page) if page % c == 0)
    vmem = pl.BlockSpec(memory_space=pltpu.VMEM)
    hbm = pl.BlockSpec(memory_space=pl.ANY)
    dma = pltpu.SemaphoreType.DMA
    return pl.pallas_call(
        functools.partial(asked_kernel, n, group, chunk),
        out_shape=[
            jax.ShapeDtypeStruct((KVH, n, unit, HD), jnp.bfloat16),
            jax.ShapeDtypeStruct((n, 2 * KVH, 128), jnp.float32),
        ],
        in_specs=[vmem, hbm, hbm],
        out_specs=[vmem, vmem],
        scratch_shapes=[
            pltpu.VMEM((KVH, n, unit, HD), jnp.bfloat16),
            pltpu.VMEM((KVH, n, unit, HD), jnp.bfloat16),
            pltpu.VMEM((2 * KVH, n, 128), jnp.float32),
            pltpu.VMEM((n, 2 * KVH, 128), jnp.float32),
            pltpu.VMEM((KVH, page, HD), jnp.bfloat16),
            pltpu.VMEM((KVH, page, HD), jnp.bfloat16),
            dma((2, KVH)), dma((KVH, n)), dma((KVH, n)), dma((KVH, n)), dma((KVH, n)),
            dma((n,)), dma((n,)),
        ],
        compiler_params=pltpu.CompilerParams(
            collective_id=1, has_side_effects=True, vmem_limit_bytes=48 * 1024 * 1024
        ),
    )(q, keys, values)


def project_kernel(n, att_ref, w_ref, out_ref, held, result, got, r_send, r_recv, l_send, l_recv, s_send, s_recv, p_send, p_recv):
    me = lax.axis_index("seq")
    rows = att_ref.shape[0]
    wide = w_ref.shape[1]
    chips = n // 2
    core = lax.rem(me, 2)
    chip = me // 2
    half = (chips + 1) // 2
    place = jnp.where(lax.rem(chip, 2) == 0, chip // 2, chips - 1 - chip // 2)

    def chip_at(p):
        p = lax.rem(p + 2 * chips, chips)
        return jnp.where(p < half, 2 * p, 2 * (chips - 1 - p) + 1)

    sibling = chip * 2 + (1 - core)
    right = chip_at(place + 1) * 2 + core
    left = chip_at(place - 1) * 2 + core

    barrier = pltpu.get_barrier_semaphore()

    @pl.loop(0, n - 1)
    def _(i):
        pl.semaphore_signal(
            barrier, inc=1, device_id={"seq": lax.rem(me + 1 + i, n)},
            device_id_type=pl.DeviceIdType.MESH,
        )

    held[pl.ds(pl.multiple_of(me * rows, rows), rows), :] = att_ref[...]
    pl.semaphore_wait(barrier, n - 1)

    def block(d):
        return held.at[pl.ds(pl.multiple_of(d * rows, rows), rows), :]

    def move(d, to, send, recv):
        return pltpu.make_async_remote_copy(
            src_ref=block(d), dst_ref=block(d), send_sem=send, recv_sem=recv,
            device_id={"seq": to}, device_id_type=pl.DeviceIdType.MESH,
        )

    def give(d, slot):
        return pltpu.make_async_remote_copy(
            src_ref=result.at[pl.ds(pl.multiple_of(d * rows, rows), rows), :],
            dst_ref=got.at[pl.ds(pl.multiple_of(me * rows, rows), rows), :],
            send_sem=p_send.at[slot], recv_sem=p_recv.at[me],
            device_id={"seq": d}, device_id_type=pl.DeviceIdType.MESH,
        )

    rights, lefts = chips // 2, (chips - 1) // 2
    started = []

    def project(c):
        return jnp.dot(
            held[pl.ds(pl.multiple_of(c * 2 * rows, 2 * rows), 2 * rows), :], w_ref[...],
            preferred_element_type=jnp.float32,
        ).astype(jnp.bfloat16)

    def finish(k, c):
        move(c * 2 + (1 - core), sibling, s_send.at[k], s_recv.at[k]).wait_recv()
        result[pl.ds(pl.multiple_of(c * 2 * rows, 2 * rows), 2 * rows), :] = project(c)
        if k == 0:
            mine = result[pl.ds(pl.multiple_of(me * rows, rows), rows), :]
            got[pl.ds(pl.multiple_of(me * rows, rows), rows), :] = mine
            sent = [give(sibling, 0)]
        else:
            sent = [give(c * 2, 2 * k), give(c * 2 + 1, 2 * k + 1)]
        for copy in sent:
            copy.start()
        started.extend(sent)

    def launch(copy):
        copy.start()
        started.append(copy)

    def step_right(s):
        launch(move(chip_at(place - s) * 2 + core, right, r_send.at[s], r_recv.at[s]))

    def step_left(s):
        launch(move(chip_at(place + s) * 2 + core, left, l_send.at[s], l_recv.at[s]))

    step_right(0)
    if lefts:
        step_left(0)
    launch(move(me, sibling, s_send.at[0], s_recv.at[0]))
    waiting = [(0, chip)]
    k = 1
    for s in range(rights):
        c = chip_at(place - 1 - s)
        move(c * 2 + core, right, r_send.at[s], r_recv.at[s]).wait_recv()
        if s + 1 < rights:
            step_right(s + 1)
        launch(move(c * 2 + core, sibling, s_send.at[k], s_recv.at[k]))
        now = [(k, c)]
        k += 1
        if s < lefts:
            c = chip_at(place + 1 + s)
            move(c * 2 + core, left, l_send.at[s], l_recv.at[s]).wait_recv()
            if s + 1 < lefts:
                step_left(s + 1)
            launch(move(c * 2 + core, sibling, s_send.at[k], s_recv.at[k]))
            now.append((k, c))
            k += 1
        for job in waiting:
            finish(*job)
        waiting = now
    for job in waiting:
        finish(*job)
    for copy in started:
        copy.wait_send()

    @pl.loop(0, n - 1)
    def _(i):
        d = lax.rem(me + 1 + i, n)
        pltpu.make_async_remote_copy(
            src_ref=result.at[pl.ds(0, rows), :],
            dst_ref=got.at[pl.ds(pl.multiple_of(d * rows, rows), rows), :],
            send_sem=p_send.at[1], recv_sem=p_recv.at[d],
            device_id={"seq": d}, device_id_type=pl.DeviceIdType.MESH,
        ).wait_recv()

    for d in range(n):
        out_ref[:, d * wide : (d + 1) * wide] = got[d * rows : (d + 1) * rows, :]


def project(attended, out_weight):
    n = lax.axis_size("seq")
    rows, features = attended.shape
    wide = out_weight.shape[1]
    chips = n // 2
    vmem = pl.BlockSpec(memory_space=pltpu.VMEM)
    dma = pltpu.SemaphoreType.DMA
    return pl.pallas_call(
        functools.partial(project_kernel, n),
        out_shape=jax.ShapeDtypeStruct((rows, n * wide), jnp.bfloat16),
        in_specs=[vmem, vmem],
        out_specs=vmem,
        scratch_shapes=[
            pltpu.VMEM((n * rows, features), jnp.bfloat16),
            pltpu.VMEM((n * rows, wide), jnp.bfloat16),
            pltpu.VMEM((n * rows, wide), jnp.bfloat16),
            dma((chips,)), dma((chips,)), dma((chips,)), dma((chips,)),
            dma((chips,)), dma((chips,)), dma((n,)), dma((n,)),
        ],
        compiler_params=pltpu.CompilerParams(
            collective_id=0, has_side_effects=True, vmem_limit_bytes=40 * 1024 * 1024
        ),
    )(attended, out_weight)


def shards(queries, new_keys, new_values, keys, values, page_list, out_weight):
    members = lax.axis_size("seq")
    tiles, width = page_list.shape
    row_total, features = queries.shape
    rows = row_total // tiles
    unit = rows * PER
    capacity = max(1, 2 * tiles * width // members)
    slots = members * capacity
    ids = jnp.arange(tiles)
    before = ids[None, :] < ids[:, None]
    matches = page_list[:, :, None, None] == page_list[None, None, :, :]
    ranking = jnp.sum(matches & before[:, None, :, None], axis=(2, 3))
    slot_index = page_list * capacity + ranking
    placing = jnp.any(
        slot_index[:, :, None] == jnp.arange(slots, dtype=jnp.int32)[None, None, :], axis=1
    ).astype(jnp.bfloat16)
    asked = queries.reshape(tiles, rows, KVH, PER, HD).transpose(0, 2, 1, 3, 4)
    asked = asked.reshape(tiles, KVH, unit, HD)
    outgoing = lax.dot_general(
        placing,
        asked.transpose(1, 0, 2, 3).reshape(KVH, tiles, unit * HD),
        (((0,), (1,)), ((), ())),
        preferred_element_type=jnp.float32,
    ).astype(jnp.bfloat16)
    outgoing = outgoing.transpose(1, 0, 2).reshape(KVH, members, capacity * unit, HD)
    got, got_stat = page_answers(outgoing, keys, values)
    a = asked.reshape(tiles, KVH, rows, PER, HD).astype(jnp.float32)
    nk = new_keys.reshape(tiles, rows, KVH, HD).transpose(0, 2, 1, 3).astype(jnp.float32)
    nv = new_values.reshape(tiles, rows, KVH, HD).transpose(0, 2, 1, 3).astype(jnp.float32)
    own_s = jnp.sum(a[:, :, :, :, None, :] * nk[:, :, None, None, :, :], axis=-1) * SCALE
    causal = jnp.arange(rows)[:, None] >= jnp.arange(rows)[None, :]
    own_s = jnp.where(causal[None, None, :, None, :], own_s, -jnp.inf)
    own_max = jnp.max(own_s, axis=-1)
    own_w = jnp.exp(own_s - own_max[..., None])
    own_total = jnp.sum(own_w, axis=-1)
    own_w = own_w.astype(jnp.bfloat16).astype(jnp.float32)
    own_sum = jnp.sum(own_w[..., None] * nv[:, :, None, None, :, :], axis=4)

    pick = slot_index[:, :, None] == jnp.arange(slots, dtype=jnp.int32)
    chosen = lax.dot_general(
        pick.reshape(tiles * width, slots).astype(jnp.bfloat16),
        got.reshape(KVH, slots, unit * HD),
        (((1,), (1,)), ((), ())),
        preferred_element_type=jnp.float32,
    ).reshape(tiles, width, KVH, rows, PER, HD)
    got_stat = got_stat[:, :, : capacity * unit].reshape(members, KVH, 2, capacity, unit)
    got_stat = got_stat.transpose(0, 3, 1, 4, 2)
    chosen_stat = jnp.sum(
        jnp.where(pick[..., None], got_stat.reshape(slots, -1)[None, None], 0.0), axis=2
    ).reshape(tiles, width, KVH, rows, PER, 2)
    chosen_max = chosen_stat[..., 0]
    chosen_total = chosen_stat[..., 1]
    top = jnp.maximum(own_max, jnp.max(chosen_max, axis=1))
    own_exp = jnp.exp(own_max - top)
    factor = chosen_total * jnp.exp(chosen_max - top[:, None])
    denom = own_exp * own_total + jnp.sum(factor, axis=1)
    numer = own_exp[..., None] * own_sum + jnp.sum(factor[..., None] * chosen, axis=1)
    attended = (numer / denom[..., None]).astype(jnp.bfloat16)
    attended = attended.transpose(0, 2, 1, 3, 4).reshape(row_total, features)
    return project(attended, out_weight)


def solution(mesh):
    rows = P(("groups", "seq"), None)
    return jax.shard_map(
        shards,
        mesh=mesh,
        in_specs=(rows, rows, rows, rows, rows, rows, P(None, "seq")),
        out_specs=rows,
        check_vma=False,
    )
```

```python
import functools
import math

import jax
import jax.numpy as jnp
from jax import lax
from jax.experimental import pallas as pl
from jax.experimental.pallas import tpu as pltpu
from jax.sharding import PartitionSpec as P

HQ = 16
KVH = 4
HD = 128
PER = HQ // KVH
SCALE = 1.0 / math.sqrt(HD)
LOG2E = math.log2(math.e)


def flash_rows(q, k_ref, v_ref, chunk):
    nt = (((1,), (1,)), ((), ()))
    count = k_ref.shape[0] // chunk
    score = lambda c: lax.dot_general(
        q, k_ref[c * chunk : (c + 1) * chunk, :], nt, preferred_element_type=jnp.float32
    )
    high = total = acc = None
    nxt = score(0)
    for c in range(count):
        s = nxt
        if c + 1 < count:
            nxt = score(c + 1)
        m = jnp.max(s, axis=1, keepdims=True)
        new = m if c == 0 else jnp.maximum(high, m)
        w = jnp.exp2((s - new) * (SCALE * LOG2E))
        t = jnp.sum(w, axis=1, keepdims=True)
        o = jnp.dot(
            w.astype(jnp.bfloat16),
            v_ref[c * chunk : (c + 1) * chunk, :],
            preferred_element_type=jnp.float32,
        )
        if c == 0:
            total, acc = t, o
        else:
            fix = jnp.exp2((high - new) * (SCALE * LOG2E))
            total = total * fix + t
            acc = acc * fix + o
        high = new
    return acc / total, high * SCALE, total


def asked_kernel(
    n, group, chunk, q_ref, k_hbm, v_hbm, got, got_stat, asked, answer, stat, stat_out, k_buf, v_buf,
    kv_sem, q_send, q_recv, o_send, o_recv, t_send, t_recv,
):
    me = lax.axis_index("seq")
    unit = q_ref.shape[2]
    blocks = n // group
    mesh_id = pl.DeviceIdType.MESH

    def page(g, src, buf, which):
        return pltpu.make_async_copy(
            src.at[:, g * HD : (g + 1) * HD], buf.at[g], kv_sem.at[which, g]
        )

    for g in range(KVH):
        page(g, k_hbm, k_buf, 0).start()
        page(g, v_hbm, v_buf, 1).start()

    barrier = pltpu.get_barrier_semaphore()

    @pl.loop(0, n - 1)
    def _(i):
        pl.semaphore_signal(
            barrier, inc=1, device_id={"seq": lax.rem(me + 1 + i, n)}, device_id_type=mesh_id
        )

    for g in range(KVH):
        asked[g, pl.ds(me, 1)] = q_ref[g, pl.ds(me, 1)]
    pl.semaphore_wait(barrier, n - 1)

    def ask(g, d):
        return pltpu.make_async_remote_copy(
            src_ref=q_ref.at[g, d], dst_ref=asked.at[g, me],
            send_sem=q_send.at[g, d], recv_sem=q_recv.at[g, me],
            device_id={"seq": d}, device_id_type=mesh_id,
        )

    def asked_by(g, d):
        return pltpu.make_async_remote_copy(
            src_ref=q_ref.at[g, d], dst_ref=asked.at[g, d],
            send_sem=q_send.at[g, d], recv_sem=q_recv.at[g, d],
            device_id={"seq": d}, device_id_type=mesh_id,
        )

    def reply(g, d):
        return pltpu.make_async_remote_copy(
            src_ref=answer.at[g, d], dst_ref=got.at[g, me],
            send_sem=o_send.at[g, d], recv_sem=o_recv.at[g, me],
            device_id={"seq": d}, device_id_type=mesh_id,
        )

    def replied_by(g, d):
        return pltpu.make_async_remote_copy(
            src_ref=answer.at[g, d], dst_ref=got.at[g, d],
            send_sem=o_send.at[g, d], recv_sem=o_recv.at[g, d],
            device_id={"seq": d}, device_id_type=mesh_id,
        )

    def note(d, slot):
        return pltpu.make_async_remote_copy(
            src_ref=stat_out.at[d], dst_ref=got_stat.at[slot],
            send_sem=t_send.at[d], recv_sem=t_recv.at[slot],
            device_id={"seq": d}, device_id_type=mesh_id,
        )

    @pl.loop(0, KVH)
    def _(g):
        @pl.loop(0, n - 1)
        def _(i):
            ask(g, lax.rem(me + 1 + i, n)).start()

    lane = lax.broadcasted_iota(jnp.int32, (group, unit, 128), 2)
    row = lax.broadcasted_iota(jnp.int32, (group, unit, 128), 1)
    diagonal = lane == row

    def line(column):
        spread = jnp.broadcast_to(column, (group * unit, 128)).reshape(group, unit, 128)
        return jnp.sum(jnp.where(diagonal, spread, 0.0), axis=1)

    for g in range(KVH):
        page(g, k_hbm, k_buf, 0).wait()
        page(g, v_hbm, v_buf, 1).wait()

        @pl.loop(0, blocks)
        def _(i):
            first = pl.multiple_of(lax.rem(me // group + i, blocks) * group, group)

            @pl.loop(0, group)
            def _(j):
                @pl.when(first + j != me)
                def _():
                    asked_by(g, first + j).wait_recv()

            q = asked[g, pl.ds(first, group)].reshape(group * unit, HD)
            out, high, total = flash_rows(q, k_buf.at[g], v_buf.at[g], chunk)
            answer[g, pl.ds(first, group)] = out.astype(jnp.bfloat16).reshape(group, unit, HD)
            stat[2 * g, pl.ds(first, group), :] = line(high)
            stat[2 * g + 1, pl.ds(first, group), :] = line(total)

            @pl.loop(0, group)
            def _(j):
                @pl.when(first + j != me)
                def _():
                    reply(g, first + j).start()

    for d in range(n):
        stat_out[d] = stat[:, d, :]

    @pl.loop(0, n - 1)
    def _(i):
        note(lax.rem(me + 1 + i, n), me).start()

    for g in range(KVH):
        got[g, pl.ds(me, 1)] = answer[g, pl.ds(me, 1)]
    got_stat[pl.ds(me, 1)] = stat_out[pl.ds(me, 1)]

    @pl.loop(0, n - 1)
    def _(i):
        d = lax.rem(me + 1 + i, n)
        for g in range(KVH):
            ask(g, d).wait_send()
            reply(g, d).wait_send()
            replied_by(g, d).wait_recv()
        note(d, d).wait_recv()
        note(d, me).wait_send()


def page_answers(q, keys, values):
    n = lax.axis_size("seq")
    unit = q.shape[2]
    page = keys.shape[0]
    group = next(b for b in (16, 8, 4, 2, 1) if n % b == 0 and b * unit <= 384)
    chunk = next(c for c in (1024, 512, page) if page % c == 0)
    vmem = pl.BlockSpec(memory_space=pltpu.VMEM)
    hbm = pl.BlockSpec(memory_space=pltpu.HBM)
    dma = pltpu.SemaphoreType.DMA
    return pl.pallas_call(
        functools.partial(asked_kernel, n, group, chunk),
        out_shape=[
            jax.ShapeDtypeStruct((KVH, n, unit, HD), jnp.bfloat16),
            jax.ShapeDtypeStruct((n, 2 * KVH, 128), jnp.float32),
        ],
        in_specs=[vmem, hbm, hbm],
        out_specs=[vmem, vmem],
        scratch_shapes=[
            pltpu.VMEM((KVH, n, unit, HD), jnp.bfloat16),
            pltpu.VMEM((KVH, n, unit, HD), jnp.bfloat16),
            pltpu.VMEM((2 * KVH, n, 128), jnp.float32),
            pltpu.VMEM((n, 2 * KVH, 128), jnp.float32),
            pltpu.VMEM((KVH, page, HD), jnp.bfloat16),
            pltpu.VMEM((KVH, page, HD), jnp.bfloat16),
            dma((2, KVH)), dma((KVH, n)), dma((KVH, n)), dma((KVH, n)), dma((KVH, n)),
            dma((n,)), dma((n,)),
        ],
        compiler_params=pltpu.CompilerParams(
            collective_id=1, has_side_effects=True, vmem_limit_bytes=48 * 1024 * 1024
        ),
    )(q, keys, values)


def project_kernel(n, att_ref, w_ref, out_ref, held, result, got, r_send, r_recv, l_send, l_recv, s_send, s_recv, p_send, p_recv):
    me = lax.axis_index("seq")
    rows = att_ref.shape[0]
    wide = w_ref.shape[1]
    chips = n // 2
    core = lax.rem(me, 2)
    chip = me // 2
    half = (chips + 1) // 2
    place = jnp.where(lax.rem(chip, 2) == 0, chip // 2, chips - 1 - chip // 2)

    def chip_at(p):
        p = lax.rem(p + 2 * chips, chips)
        return jnp.where(p < half, 2 * p, 2 * (chips - 1 - p) + 1)

    sibling = chip * 2 + (1 - core)
    right = chip_at(place + 1) * 2 + core
    left = chip_at(place - 1) * 2 + core

    barrier = pltpu.get_barrier_semaphore()

    @pl.loop(0, n - 1)
    def _(i):
        pl.semaphore_signal(
            barrier, inc=1, device_id={"seq": lax.rem(me + 1 + i, n)},
            device_id_type=pl.DeviceIdType.MESH,
        )

    held[pl.ds(pl.multiple_of(me * rows, rows), rows), :] = att_ref[...]
    pl.semaphore_wait(barrier, n - 1)

    def block(d):
        return held.at[pl.ds(pl.multiple_of(d * rows, rows), rows), :]

    def move(d, to, send, recv):
        return pltpu.make_async_remote_copy(
            src_ref=block(d), dst_ref=block(d), send_sem=send, recv_sem=recv,
            device_id={"seq": to}, device_id_type=pl.DeviceIdType.MESH,
        )

    def give(d, slot):
        return pltpu.make_async_remote_copy(
            src_ref=result.at[pl.ds(pl.multiple_of(d * rows, rows), rows), :],
            dst_ref=got.at[pl.ds(pl.multiple_of(me * rows, rows), rows), :],
            send_sem=p_send.at[slot], recv_sem=p_recv.at[me],
            device_id={"seq": d}, device_id_type=pl.DeviceIdType.MESH,
        )

    full = (chips - 1) // 2
    hops = chips // 2
    started = []

    def project(c):
        return jnp.dot(
            held[pl.ds(pl.multiple_of(c * 2 * rows, 2 * rows), 2 * rows), :], w_ref[...],
            preferred_element_type=jnp.float32,
        ).astype(jnp.bfloat16)

    def finish(k, c):
        move(c * 2 + (1 - core), sibling, s_send.at[k], s_recv.at[k]).wait_recv()
        result[pl.ds(pl.multiple_of(c * 2 * rows, 2 * rows), 2 * rows), :] = project(c)
        if k == 0:
            mine = result[pl.ds(pl.multiple_of(me * rows, rows), rows), :]
            got[pl.ds(pl.multiple_of(me * rows, rows), rows), :] = mine
            sent = [give(sibling, 0)]
        else:
            sent = [give(c * 2, 2 * k), give(c * 2 + 1, 2 * k + 1)]
        for copy in sent:
            copy.start()
        started.extend(sent)

    def launch(copy):
        copy.start()
        started.append(copy)

    piece = held.shape[1] // 2

    def hop(c, side, s, p):
        part = held.at[
            pl.ds(pl.multiple_of((c * 2 + core) * rows, rows), rows), p * piece : (p + 1) * piece
        ]
        send, recv, to = (r_send, r_recv, right) if side > 0 else (l_send, l_recv, left)
        return pltpu.make_async_remote_copy(
            src_ref=part, dst_ref=part, send_sem=send.at[s, p], recv_sem=recv.at[s, p],
            device_id={"seq": to}, device_id_type=pl.DeviceIdType.MESH,
        )

    def pieces(side, s):
        return (0, 1) if s < full else (0,) if side > 0 else (1,)

    if hops:
        for p in (0, 1):
            for side in (1, -1):
                if p in pieces(side, 0):
                    launch(hop(chip, side, 0, p))
    launch(move(me, sibling, s_send.at[0], s_recv.at[0]))
    waiting = [(0, chip)]
    k = 1
    for s in range(hops):
        for p in (0, 1):
            for side in (1, -1):
                c = chip_at(place - side * (1 + s))
                if p in pieces(side, s):
                    hop(c, side, s, p).wait_recv()
                if s + 1 < hops and p in pieces(side, s + 1):
                    launch(hop(c, side, s + 1, p))
        now = []
        for side in (1, -1) if s < full else (1,):
            c = chip_at(place - side * (1 + s))
            launch(move(c * 2 + core, sibling, s_send.at[k], s_recv.at[k]))
            now.append((k, c))
            k += 1
        for job in waiting:
            finish(*job)
        waiting = now
    for job in waiting:
        finish(*job)
    for copy in started:
        copy.wait_send()

    @pl.loop(0, n - 1)
    def _(i):
        d = lax.rem(me + 1 + i, n)
        pltpu.make_async_remote_copy(
            src_ref=result.at[pl.ds(0, rows), :],
            dst_ref=got.at[pl.ds(pl.multiple_of(d * rows, rows), rows), :],
            send_sem=p_send.at[1], recv_sem=p_recv.at[d],
            device_id={"seq": d}, device_id_type=pl.DeviceIdType.MESH,
        ).wait_recv()

    for d in range(n):
        out_ref[:, d * wide : (d + 1) * wide] = got[d * rows : (d + 1) * rows, :]


def project(attended, out_weight):
    n = lax.axis_size("seq")
    rows, features = attended.shape
    wide = out_weight.shape[1]
    chips = n // 2
    vmem = pl.BlockSpec(memory_space=pltpu.VMEM)
    dma = pltpu.SemaphoreType.DMA
    return pl.pallas_call(
        functools.partial(project_kernel, n),
        out_shape=jax.ShapeDtypeStruct((rows, n * wide), jnp.bfloat16),
        in_specs=[vmem, vmem],
        out_specs=vmem,
        scratch_shapes=[
            pltpu.VMEM((n * rows, features), jnp.bfloat16),
            pltpu.VMEM((n * rows, wide), jnp.bfloat16),
            pltpu.VMEM((n * rows, wide), jnp.bfloat16),
            dma((chips, 2)), dma((chips, 2)), dma((chips, 2)), dma((chips, 2)),
            dma((chips,)), dma((chips,)), dma((n,)), dma((n,)),
        ],
        compiler_params=pltpu.CompilerParams(
            collective_id=0, has_side_effects=True, vmem_limit_bytes=40 * 1024 * 1024
        ),
    )(attended, out_weight)


def shards(queries, new_keys, new_values, keys, values, page_list, out_weight):
    members = lax.axis_size("seq")
    tiles, width = page_list.shape
    row_total, features = queries.shape
    rows = row_total // tiles
    unit = rows * PER
    capacity = max(1, 2 * tiles * width // members)
    slots = members * capacity
    ids = jnp.arange(tiles)
    before = ids[None, :] < ids[:, None]
    matches = page_list[:, :, None, None] == page_list[None, None, :, :]
    ranking = jnp.sum(matches & before[:, None, :, None], axis=(2, 3))
    slot_index = page_list * capacity + ranking
    placing = jnp.any(
        slot_index[:, :, None] == jnp.arange(slots, dtype=jnp.int32)[None, None, :], axis=1
    ).astype(jnp.bfloat16)
    asked = queries.reshape(tiles, rows, KVH, PER, HD).transpose(0, 2, 1, 3, 4)
    asked = asked.reshape(tiles, KVH, unit, HD)
    outgoing = lax.dot_general(
        placing,
        asked.transpose(1, 0, 2, 3).reshape(KVH, tiles, unit * HD),
        (((0,), (1,)), ((), ())),
        preferred_element_type=jnp.float32,
    ).astype(jnp.bfloat16)
    outgoing = outgoing.transpose(1, 0, 2).reshape(KVH, members, capacity * unit, HD)
    got, got_stat = page_answers(outgoing, keys, values)
    a = asked.reshape(tiles, KVH, rows, PER, HD).astype(jnp.float32)
    nk = new_keys.reshape(tiles, rows, KVH, HD).transpose(0, 2, 1, 3).astype(jnp.float32)
    nv = new_values.reshape(tiles, rows, KVH, HD).transpose(0, 2, 1, 3).astype(jnp.float32)
    own_s = jnp.sum(a[:, :, :, :, None, :] * nk[:, :, None, None, :, :], axis=-1) * SCALE
    causal = jnp.arange(rows)[:, None] >= jnp.arange(rows)[None, :]
    own_s = jnp.where(causal[None, None, :, None, :], own_s, -jnp.inf)
    own_max = jnp.max(own_s, axis=-1)
    own_w = jnp.exp(own_s - own_max[..., None])
    own_total = jnp.sum(own_w, axis=-1)
    own_w = own_w.astype(jnp.bfloat16).astype(jnp.float32)
    own_sum = jnp.sum(own_w[..., None] * nv[:, :, None, None, :, :], axis=4)

    pick = slot_index[:, :, None] == jnp.arange(slots, dtype=jnp.int32)
    chosen = lax.dot_general(
        pick.reshape(tiles * width, slots).astype(jnp.bfloat16),
        got.reshape(KVH, slots, unit * HD),
        (((1,), (1,)), ((), ())),
        preferred_element_type=jnp.float32,
    ).reshape(tiles, width, KVH, rows, PER, HD)
    got_stat = got_stat[:, :, : capacity * unit].reshape(members, KVH, 2, capacity, unit)
    got_stat = got_stat.transpose(0, 3, 1, 4, 2)
    chosen_stat = jnp.sum(
        jnp.where(pick[..., None], got_stat.reshape(slots, -1)[None, None], 0.0), axis=2
    ).reshape(tiles, width, KVH, rows, PER, 2)
    chosen_max = chosen_stat[..., 0]
    chosen_total = chosen_stat[..., 1]
    top = jnp.maximum(own_max, jnp.max(chosen_max, axis=1))
    own_exp = jnp.exp(own_max - top)
    factor = chosen_total * jnp.exp(chosen_max - top[:, None])
    denom = own_exp * own_total + jnp.sum(factor, axis=1)
    numer = own_exp[..., None] * own_sum + jnp.sum(factor[..., None] * chosen, axis=1)
    attended = (numer / denom[..., None]).astype(jnp.bfloat16)
    attended = attended.transpose(0, 2, 1, 3, 4).reshape(row_total, features)
    return project(attended, out_weight)


def solution(mesh):
    rows = P(("groups", "seq"), None)
    return jax.shard_map(
        shards,
        mesh=mesh,
        in_specs=(rows, rows, rows, rows, rows, rows, P(None, "seq")),
        out_specs=rows,
        check_vma=False,
    )
```
